32 devices in a mesh: rep: 8 (over y, x, core), fsdp: 4 (over z).
Axes of the slice: x: 2, y: 2, z: 4, core: 2. Of those that a mesh axis runs over, the one named last changes fastest.
Arguments:
- replica_inner_weight: bfloat16 [8, 512, 16384], P('rep', 'fsdp'), may hold values from -30 to 30
- outer_weights: float32 [512, 16384], P('fsdp'), may hold values from -6 to 6
- momentum: float32 [512, 16384], P('fsdp', 'rep'), may hold values from -4 to 4
- exponents: int32 [8, 512, 128], P('rep', 'fsdp'), may hold values from 0 to 2
- levels: int32 [16], replicated, may hold values from -60 to 60, as said below
Outputs:
- inner_next: bfloat16 [8, 512, 16384], P('rep', 'fsdp')
- momentum_next: float32 [512, 16384], P('fsdp', 'rep')
- outer_next: float32 [512, 16384], P('fsdp', 'rep')
The draws below stay inside these ranges and needn't reach their ends.
Inputs may be any that keep to these rules, and one draw needn't show every extreme that they name: `levels`: 16 distinct values, half of them negative and half positive, ascending.
All inputs are finite; a program needn't handle non-finite values. Where the reference program divides by a largest or mean magnitude, that divisor is 1e-20 or more.
Results may differ from the reference program's by a relative error of at most 0.0085.
Values may be sent and summed in bfloat16 or wider, within the bound.
A program may use at most 128 MiB of HBM per device.

```python
import jax
import jax.numpy as jnp
from jax import lax

D = 16384
BLOCK = 128
NLEV = 16
ROWS = 512
REPS = 8


def draw_levels(key, part):
    base_key = jax.random.fold_in(key, 11)
    first_key, second_key = jax.random.split(base_key)
    negative = jax.random.permutation(first_key, 60)[:NLEV // 2] + 1
    positive = jax.random.permutation(second_key, 60)[:NLEV // 2] + 1
    values = jnp.concatenate([-negative, positive])
    return jnp.sort(values).astype(jnp.int32)


def weight_fields(key):
    base_key = jax.random.fold_in(key, 23)
    outer_key, noise_key = jax.random.split(base_key, 2)
    outer_field = jnp.clip(jax.random.normal(outer_key, (ROWS, D), jnp.float32), -6.0, 6.0)
    noise = jnp.clip(jax.random.normal(noise_key, (REPS, ROWS, D), jnp.float32), -6.0, 6.0)
    position = jnp.arange(ROWS, dtype=jnp.float32) / jnp.float32(max(ROWS - 1, 1))
    column_place = jnp.arange(D, dtype=jnp.float32) / jnp.float32(max(D - 1, 1))
    row_scale = 0.12 * jnp.exp(position * jnp.log(8.0))
    column_scale = 0.5 * jnp.exp(column_place * jnp.log(4.0))
    spread = row_scale[:, None] * column_scale[None, :]
    inner_field = jnp.clip(outer_field[None] - spread[None] * noise, -30.0, 30.0)
    return (outer_field, inner_field)


def draw_outer_weights(key, part):
    return weight_fields(key)[0].astype(jnp.float32)


def draw_replica_inner_weight(key, part):
    return weight_fields(key)[1].astype(jnp.bfloat16)


def touch_ends(array, rng, smallest, high):
    extent = array.shape
    spot = [jax.random.randint(jax.random.fold_in(rng, axis), (), 0, extent[axis]) for axis in range(len(extent))]
    array = array.at[tuple(spot)].set(smallest)
    longest = extent.index(max(extent))
    spot[longest] = (spot[longest] + 1) % extent[longest]
    return array.at[tuple(spot)].set(high)


def steps_of(rng, shape, shards, least, largest):
    loudness, own = 1.0, jax.random.fold_in(rng, 6)
    for dim, shards_of in shards:
        steps = jnp.exp(jax.random.uniform(jax.random.fold_in(own, dim), (shards_of,), jnp.float32, least / len(shards), largest / len(shards)))
        loudness = loudness * jnp.repeat(steps, shape[dim] // shards_of).reshape([-1 if axis == dim else 1 for axis in range(len(shape))])
    return loudness


def scatter_about(key, shape, deviation, most, cuts=(), kind=jnp.bfloat16):
    entries = jax.random.normal(key, shape, jnp.float32) * deviation
    if len(cuts) > 0:
        entries = steps_of(key, shape, cuts, -0.22, 0.18) * entries
    return jnp.clip(entries, min=-most, max=most).astype(kind)


def setup_inputs(seed: int = 0) -> dict:
    arg_keys = jax.random.split(jax.random.key(seed), 6)
    replica_inner_weight = draw_replica_inner_weight(jax.random.fold_in(arg_keys[5], 71), 0)
    outer_weights = draw_outer_weights(jax.random.fold_in(arg_keys[5], 71), 0)
    momentum = scatter_about(arg_keys[2], (ROWS, D), 0.3, 4.0, ((0, 4), (1, 8)), jnp.float32)
    exponents = touch_ends(jax.random.randint(arg_keys[3], (REPS, ROWS, D // BLOCK), 0, 3), jax.random.fold_in(arg_keys[3], 1), 0, 2).astype(jnp.int32)
    levels = draw_levels(jax.random.fold_in(arg_keys[5], 71), 0)
    return {"replica_inner_weight": replica_inner_weight, "outer_weights": outer_weights, "momentum": momentum, "exponents": exponents, "levels": levels}


softness_factor = 0.02
clip_rms = 0.1
outer_rate = 0.7
outer_mu = 0.9
mix_rate = 0.5

def encode_grad(pseudo_grad, exponents, levels):
    quantize_grid_points = levels.astype(jnp.float32) / jnp.max(jnp.abs(levels)).astype(jnp.float32)
    block_scale = jnp.exp2(exponents.astype(jnp.float32))[..., None]
    row_count = pseudo_grad.shape[0]
    rescaled_gradient = pseudo_grad.reshape(row_count, exponents.shape[-1], -1) / block_scale
    closest_grid_level = (rescaled_gradient - quantize_grid_points[0]) ** 2
    for grid_level_index in range(1, NLEV):
        closest_grid_level = jnp.minimum(closest_grid_level, (rescaled_gradient - quantize_grid_points[grid_level_index]) ** 2)
    weighted = jnp.zeros_like(rescaled_gradient)
    weights_sum = jnp.zeros_like(rescaled_gradient)
    for grid_level_index in range(NLEV):
        current_weight = jnp.exp(-((rescaled_gradient - quantize_grid_points[grid_level_index]) ** 2 - closest_grid_level) / softness_factor)
        weighted = weighted + current_weight * quantize_grid_points[grid_level_index]
        weights_sum = weights_sum + current_weight
    coded = block_scale * weighted / weights_sum
    return coded.reshape(row_count, -1).astype(jnp.bfloat16)

def reference(replica_inner_weight, outer_weights, momentum, exponents, levels):
    replicas = replica_inner_weight.shape[0]

    def accumulate(running, items):
        inner_one, expo_one = items
        coded = encode_grad(outer_weights - inner_one.astype(jnp.float32), expo_one, levels)
        return (running + coded.astype(jnp.float32), None)
    running = lax.scan(accumulate, jnp.zeros(outer_weights.shape, jnp.float32), (replica_inner_weight, exponents))[0]
    mean_grad = running / jnp.float32(replicas)
    mean_square = jnp.sum(mean_grad * mean_grad) / jnp.float32(mean_grad.size)
    clip = jnp.minimum(jnp.float32(1.0), clip_rms / jnp.sqrt(mean_square + 1e-06))
    grad = clip * mean_grad
    momentum_next = outer_mu * momentum + grad
    outer_next = outer_weights - outer_rate * (grad + outer_mu * momentum_next)
    outer_half = outer_next.astype(jnp.bfloat16)

    def blend(inner_one):
        return (mix_rate * outer_half.astype(jnp.float32) + (1.0 - mix_rate) * inner_one.astype(jnp.float32)).astype(jnp.bfloat16)
    inner_next = lax.map(blend, replica_inner_weight)
    return (inner_next, momentum_next, outer_next)
```

```python
import functools
import math

import jax
import jax.numpy as jnp
from jax import lax
from jax.experimental import pallas as pl
from jax.experimental.pallas import tpu as pltpu
from jax.sharding import PartitionSpec as P

NLEV = 16
BLOCK = 128
ROWS_AT_ONCE = 32
CHUNKS = 4

softness_factor = 0.02
clip_rms = 0.1
outer_rate = 0.7
outer_mu = 0.9
mix_rate = 0.5

SHARP = math.sqrt(math.log2(math.e) / softness_factor)


def other_chip(q, s, chips):
    t = q
    bit = 1
    while bit < chips:
        if s & bit:
            t = t + bit * (1 - 2 * (lax.div(q, bit) % 2))
        bit *= 2
    return t


def kernel(
    reps, groups, entries,
    inner_hbm, outer_hbm, mom_hbm, expo_hbm, levels_ref,
    next_hbm, mom_next_hbm, outer_next_hbm,
    inner_v, outer_v, mom_v, expo_v, scale_v, coded_sib, coded_own, from_sib, from_chip,
    mean_v, half_v, mom_out, outer_out, parts,
    in_sem, sib_send, sib_recv, chip_send, chip_recv, part_send, part_recv,
    own_send, own_recv, fwd_send, fwd_recv, out_sem, flat_sem,
):
    chips = reps // 2
    rep = lax.axis_index("rep")
    group = lax.axis_index("fsdp")
    core = lax.rem(rep, 2)
    chip = lax.div(rep, 2)
    rows, width = mom_v.shape
    blocks = width // BLOCK
    sibling = {"rep": chip * 2 + 1 - core}
    order = list(range(chips - 1, -1, -1))
    chip_of = [other_chip(chip, s, chips) for s in range(chips)]
    peer = [{"rep": 2 * chip_of[s] + core} for s in range(chips)]
    across = [{"fsdp": lax.rem(group + s, groups)} for s in range(groups)]

    def piece(v):
        return 2 * chip_of[v // 2] + (core if v % 2 else 1 - core)

    def columns(v):
        return pl.ds(pl.multiple_of(piece(v) * width, BLOCK), width)

    expo_in = pltpu.make_async_copy(expo_hbm.at[0], expo_v, in_sem.at[2 * reps])
    expo_in.start()
    loads = {}
    for s in order:
        for v in (2 * s, 2 * s + 1):
            a = pltpu.make_async_copy(inner_hbm.at[0, :, columns(v)], inner_v.at[v], in_sem.at[2 * v])
            b = pltpu.make_async_copy(outer_hbm.at[:, columns(v)], outer_v.at[v], in_sem.at[2 * v + 1])
            a.start()
            b.start()
            loads[v] = (a, b)
    mom_in = pltpu.make_async_copy(mom_hbm, mom_v, in_sem.at[2 * reps + 1])
    mom_in.start()

    barrier = pltpu.get_barrier_semaphore()
    partners = [sibling] + peer[1:] + across[1:]
    for who in partners:
        pl.semaphore_signal(barrier, inc=1, device_id=who, device_id_type=pl.DeviceIdType.MESH)
    pl.semaphore_wait(barrier, len(partners))

    def send(src, dst, send_sem, recv_sem, who):
        copy = pltpu.make_async_remote_copy(
            src_ref=src, dst_ref=dst, send_sem=send_sem, recv_sem=recv_sem,
            device_id=who, device_id_type=pl.DeviceIdType.MESH,
        )
        copy.start()
        return copy

    most = jnp.abs(levels_ref[0])
    for k in range(1, NLEV):
        most = jnp.maximum(most, jnp.abs(levels_ref[k]))
    unit = jnp.max(SHARP / jnp.full((8, BLOCK), most.astype(jnp.float32)))
    grid = [levels_ref[k].astype(jnp.float32) * unit for k in range(NLEV)]

    expo_in.wait()
    expo = expo_v[...].astype(jnp.float32)
    scale_v[0] = jnp.exp2(expo).astype(jnp.bfloat16)
    scale_v[1] = jnp.exp2(-expo).astype(jnp.bfloat16)

    def encode(v, dst):
        first = piece(v) * blocks

        def one(b, carry):
            pick = (
                lax.broadcasted_iota(jnp.int32, (expo_v.shape[1], BLOCK), 0) == first + b
            ).astype(jnp.bfloat16)
            scale = jnp.dot(scale_v[0], pick, preferred_element_type=jnp.float32)
            inverse = jnp.dot(scale_v[1], pick, preferred_element_type=jnp.float32)
            cols = pl.ds(pl.multiple_of(b * BLOCK, BLOCK), BLOCK)
            for r in range(0, rows, ROWS_AT_ONCE):
                at = slice(r, r + ROWS_AT_ONCE)
                pseudo = outer_v[v, at, cols] - inner_v[v, at, cols].astype(jnp.float32)
                u = pseudo * (inverse[at] * SHARP)
                near = jnp.clip(u, grid[0], grid[NLEV - 1])
                far = 2.0 * u - near
                num = den = None
                for k in range(NLEV):
                    w = jnp.exp2((grid[k] - near) * (far - grid[k]))
                    num = w * grid[k] if num is None else num + w * grid[k]
                    den = w if den is None else den + w
                coded = scale[at] * (1.0 / SHARP) * num / den
                dst[at, cols] = coded.astype(jnp.bfloat16)
            return carry

        lax.fori_loop(0, blocks, one, 0)

    def over_blocks(body, init=0):
        return lax.fori_loop(
            0, blocks, lambda b, c: body(pl.ds(pl.multiple_of(b * BLOCK, BLOCK), BLOCK), c), init
        )

    f32 = jnp.float32
    pending = []
    from_sib_copies, from_chip_copies = {}, {}

    def pair_sum(s):
        from_sib_copies[s].wait_recv()
        if s == 0:
            return

        def body(cols, c):
            coded_own[s, :, cols] = (
                coded_own[s, :, cols].astype(f32) + from_sib[s, :, cols].astype(f32)
            ).astype(jnp.bfloat16)
            return c

        over_blocks(body)
        from_chip_copies[s] = send(
            coded_own.at[s], from_chip.at[s - 1], chip_send.at[s - 1], chip_recv.at[s - 1], peer[s]
        )

    for s in order:
        for v, dst in ((2 * s, coded_sib.at[s]), (2 * s + 1, coded_own.at[s])):
            for load in loads[v]:
                load.wait()
            encode(v, dst)
            if v % 2 == 0:
                from_sib_copies[s] = send(
                    coded_sib.at[s], from_sib.at[s], sib_send.at[s], sib_recv.at[s], sibling
                )
        pair_sum(s)
    for s in order[:-1]:
        from_chip_copies[s].wait_recv()

    def add_up(cols, acc):
        total = coded_own[0, :, cols].astype(f32) + from_sib[0, :, cols].astype(f32)
        for s in range(1, chips):
            total = total + from_chip[s - 1, :, cols].astype(f32)
        mean = total / f32(reps)
        mean_v[:, cols] = mean
        return acc + jnp.sum((mean * mean).reshape(rows // 8, 8, BLOCK), axis=0)

    parts[0] = over_blocks(add_up, jnp.zeros((8, BLOCK), f32))
    slot = 3
    sem = 0
    for stage, who in enumerate(([sibling], peer[1:], across[1:])):
        copies = []
        for i, one in enumerate(who):
            copies.append(
                send(parts.at[stage], parts.at[slot + i], part_send.at[sem + i], part_recv.at[sem + i], one)
            )
        total = parts[stage]
        for i, copy in enumerate(copies):
            copy.wait()
            total = total + parts[slot + i]
        slot += len(who)
        sem += len(who)
        if stage < 2:
            parts[stage + 1] = total
    squares = jnp.full((8, BLOCK), jnp.sum(total))
    clip = jnp.max(
        jnp.minimum(f32(1.0), clip_rms / jnp.sqrt(squares / f32(entries) + 1e-06))
    )

    tall = rows // CHUNKS
    mom_in.wait()
    own_copies, fwd_copies, outs = {}, {}, []

    def forward(s, c):
        v = 2 * s + 1
        at = pl.ds(c * tall, tall)
        fwd_copies[s, c] = send(
            half_v.at[v, at], half_v.at[v - 1, at],
            fwd_send.at[s * CHUNKS + c], fwd_recv.at[s * CHUNKS + c], sibling,
        )

    def mix(v, c):
        at = pl.ds(c * tall, tall)

        def body(cols, carry):
            inner_v[v, at, cols] = (
                mix_rate * half_v[v, at, cols].astype(f32)
                + (1.0 - mix_rate) * inner_v[v, at, cols].astype(f32)
            ).astype(jnp.bfloat16)
            return carry

        over_blocks(body)
        out = pltpu.make_async_copy(
            inner_v.at[v, at], next_hbm.at[0, at, columns(v)], out_sem.at[v * CHUNKS + c]
        )
        out.start()
        outs.append(out)

    for c in range(CHUNKS):
        at = pl.ds(c * tall, tall)

        def step(cols, carry):
            grad = clip * mean_v[at, cols]
            mom = outer_mu * mom_v[at, cols] + grad
            new = outer_v[1, at, cols] - outer_rate * (grad + outer_mu * mom)
            mom_out[at, cols] = mom
            outer_out[at, cols] = new
            half_v[1, at, cols] = new.astype(jnp.bfloat16)
            return carry

        over_blocks(step)
        for s in order[:-1]:
            i = (s - 1) * CHUNKS + c
            own_copies[s, c] = send(
                half_v.at[1, at], half_v.at[2 * s + 1, at], own_send.at[i], own_recv.at[i], peer[s]
            )
        forward(0, c)
    for i, (src, dst) in enumerate(((mom_out, mom_next_hbm), (outer_out, outer_next_hbm))):
        out = pltpu.make_async_copy(src, dst, flat_sem.at[i])
        out.start()
        outs.append(out)
    for c in range(CHUNKS):
        mix(1, c)
    for c in range(CHUNKS):
        fwd_copies[0, c].wait_recv()
        mix(0, c)
    last = None
    for c in range(CHUNKS):
        for s in order[-2::-1]:
            own_copies[s, c].wait_recv()
            forward(s, c)
            mix(2 * s + 1, c)
            if last is not None:
                fwd_copies[last].wait_recv()
                mix(2 * last[0], last[1])
            last = (s, c)
    if last is not None:
        fwd_copies[last].wait_recv()
        mix(2 * last[0], last[1])

    for copies in (from_sib_copies, from_chip_copies, own_copies, fwd_copies):
        for copy in copies.values():
            copy.wait_send()
    for out in outs:
        out.wait()


def per_device(inner, outer, momentum, exponents, levels):
    reps = lax.axis_size("rep")
    groups = lax.axis_size("fsdp")
    chips = reps // 2
    rows, columns = outer.shape
    width = momentum.shape[1]
    n_parts = 1 + (chips - 1) + (groups - 1)
    bf16, f32 = jnp.bfloat16, jnp.float32
    dma = pltpu.SemaphoreType.DMA
    hbm = pl.BlockSpec(memory_space=pl.ANY)
    return pl.pallas_call(
        functools.partial(kernel, reps, groups, rows * groups * columns),
        out_shape=(
            jax.ShapeDtypeStruct(inner.shape, inner.dtype),
            jax.ShapeDtypeStruct(momentum.shape, f32),
            jax.ShapeDtypeStruct(momentum.shape, f32),
        ),
        in_specs=[hbm] * 4 + [pl.BlockSpec(memory_space=pltpu.SMEM)],
        out_specs=(hbm,) * 3,
        scratch_shapes=[
            pltpu.VMEM((reps, rows, width), bf16),
            pltpu.VMEM((reps, rows, width), f32),
            pltpu.VMEM((rows, width), f32),
            pltpu.VMEM(exponents.shape[1:], jnp.int32),
            pltpu.VMEM((2,) + exponents.shape[1:], bf16),
            pltpu.VMEM((chips, rows, width), bf16),
            pltpu.VMEM((chips, rows, width), bf16),
            pltpu.VMEM((chips, rows, width), bf16),
            pltpu.VMEM((chips - 1, rows, width), bf16),
            pltpu.VMEM((rows, width), f32),
            pltpu.VMEM((reps, rows, width), bf16),
            pltpu.VMEM((rows, width), f32),
            pltpu.VMEM((rows, width), f32),
            pltpu.VMEM((3 + n_parts, 8, BLOCK), f32),
            dma((2 * reps + 2,)),
            dma((chips,)),
            dma((chips,)),
            dma((chips - 1,)),
            dma((chips - 1,)),
            dma((n_parts,)),
            dma((n_parts,)),
            dma(((chips - 1) * CHUNKS,)),
            dma(((chips - 1) * CHUNKS,)),
            dma((chips * CHUNKS,)),
            dma((chips * CHUNKS,)),
            dma((reps * CHUNKS,)),
            dma((2,)),
        ],
        compiler_params=pltpu.CompilerParams(
            collective_id=0, has_side_effects=True, vmem_limit_bytes=56 * 1024 * 1024
        ),
        cost_estimate=pl.CostEstimate(
            flops=100 * rows * columns,
            bytes_accessed=8 * rows * columns + 16 * rows * width,
            transcendentals=NLEV * rows * columns,
        ),
    )(inner, outer, momentum, exponents, levels)


def solution(mesh):
    placed = (
        P("rep", "fsdp", None),
        P("fsdp", None),
        P("fsdp", "rep"),
        P("rep", "fsdp", None),
        P(),
    )
    return jax.shard_map(
        per_device,
        mesh=mesh,
        in_specs=placed,
        out_specs=(P("rep", "fsdp", None), P("fsdp", "rep"), P("fsdp", "rep")),
        check_vma=False,
    )
```

```python
import functools
import math

import jax
import jax.numpy as jnp
from jax import lax
from jax.experimental import pallas as pl
from jax.experimental.pallas import tpu as pltpu
from jax.sharding import PartitionSpec as P

NLEV = 16
BLOCK = 128
ROWS_AT_ONCE = 32
CHUNKS = 4

softness_factor = 0.02
clip_rms = 0.1
outer_rate = 0.7
outer_mu = 0.9
mix_rate = 0.5

SHARP = math.sqrt(math.log2(math.e) / softness_factor)


def other_chip(q, s, chips):
    t = q
    bit = 1
    while bit < chips:
        if s & bit:
            t = t + bit * (1 - 2 * (lax.div(q, bit) % 2))
        bit *= 2
    return t


def kernel(
    reps, groups, entries,
    inner_hbm, outer_hbm, mom_hbm, expo_hbm, levels_ref,
    next_hbm, mom_next_hbm, outer_next_hbm,
    inner_v, outer_v, mom_v, expo_v, scale_v, coded_sib, coded_own, from_sib, from_chip,
    mean_v, half_v, mom_out, outer_out, parts,
    in_sem, sib_send, sib_recv, chip_send, chip_recv, part_send, part_recv,
    own_send, own_recv, fwd_send, fwd_recv, out_sem, flat_sem,
):
    chips = reps // 2
    rep = lax.axis_index("rep")
    group = lax.axis_index("fsdp")
    core = lax.rem(rep, 2)
    chip = lax.div(rep, 2)
    rows, width = mom_v.shape
    blocks = width // BLOCK
    broad = math.gcd(width, 8 * BLOCK)
    sibling = {"rep": chip * 2 + 1 - core}
    order = list(range(chips - 1, -1, -1))
    chip_of = [other_chip(chip, s, chips) for s in range(chips)]
    peer = [{"rep": 2 * chip_of[s] + core} for s in range(chips)]
    across = [{"fsdp": lax.rem(group + s, groups)} for s in range(groups)]

    def piece(v):
        return 2 * chip_of[v // 2] + (core if v % 2 else 1 - core)

    def columns(v):
        return pl.ds(pl.multiple_of(piece(v) * width, BLOCK), width)

    expo_in = pltpu.make_async_copy(expo_hbm.at[0], expo_v, in_sem.at[2 * reps])
    expo_in.start()
    loads = {}
    for s in order:
        for v in (2 * s, 2 * s + 1):
            a = pltpu.make_async_copy(inner_hbm.at[0, :, columns(v)], inner_v.at[v], in_sem.at[2 * v])
            b = pltpu.make_async_copy(outer_hbm.at[:, columns(v)], outer_v.at[v], in_sem.at[2 * v + 1])
            a.start()
            b.start()
            loads[v] = (a, b)
    mom_in = pltpu.make_async_copy(mom_hbm, mom_v, in_sem.at[2 * reps + 1])
    mom_in.start()

    barrier = pltpu.get_barrier_semaphore()
    near_by = [sibling] + peer[1:] + [
        {"rep": 2 * chip_of[s] + 1 - core} for s in range(1, chips)
    ]
    partners = near_by + across[1:]
    for who in partners:
        pl.semaphore_signal(barrier, inc=1, device_id=who, device_id_type=pl.DeviceIdType.MESH)
    pl.semaphore_wait(barrier, len(partners))

    def send(src, dst, send_sem, recv_sem, who):
        copy = pltpu.make_async_remote_copy(
            src_ref=src, dst_ref=dst, send_sem=send_sem, recv_sem=recv_sem,
            device_id=who, device_id_type=pl.DeviceIdType.MESH,
        )
        copy.start()
        return copy

    most = jnp.abs(levels_ref[0])
    for k in range(1, NLEV):
        most = jnp.maximum(most, jnp.abs(levels_ref[k]))
    unit = jnp.max(SHARP / jnp.full((8, BLOCK), most.astype(jnp.float32)))
    grid = [levels_ref[k].astype(jnp.float32) * unit for k in range(NLEV)]

    expo_in.wait()
    expo = expo_v[...].astype(jnp.float32)
    scale_v[0] = jnp.exp2(expo).astype(jnp.bfloat16)
    scale_v[1] = jnp.exp2(-expo).astype(jnp.bfloat16)

    f32 = jnp.float32

    def encode(v, dst):
        first = piece(v) * blocks

        def scales(b):
            pick = (
                lax.broadcasted_iota(jnp.int32, (expo_v.shape[1], BLOCK), 0) == first + b
            ).astype(jnp.bfloat16)
            return tuple(
                jnp.dot(scale_v[i], pick, preferred_element_type=jnp.float32) for i in range(2)
            )

        def one(b, carry):
            scale, inverse = carry
            later = scales(b + 1)
            cols = pl.ds(pl.multiple_of(b * BLOCK, BLOCK), BLOCK)
            for r in range(0, rows, ROWS_AT_ONCE):
                at = slice(r, r + ROWS_AT_ONCE)
                pseudo = outer_v[v, at, cols] - inner_v[v, at, cols].astype(jnp.float32)
                u = pseudo * (inverse[at] * SHARP)
                near = jnp.clip(u, grid[0], grid[NLEV - 1])
                far = 2.0 * u - near
                num = den = None
                for k in range(NLEV):
                    w = jnp.exp2(((grid[k] - near) * (far - grid[k])).astype(jnp.bfloat16))
                    wg = w * grid[k].astype(jnp.bfloat16)
                    some_num = wg if k % 4 == 0 else some_num + wg
                    some_den = w if k % 4 == 0 else some_den + w
                    if k % 4 == 3:
                        some_num, some_den = some_num.astype(f32), some_den.astype(f32)
                        num = some_num if num is None else num + some_num
                        den = some_den if den is None else den + some_den
                guess = pl.reciprocal(den, approx=True)
                guess = guess * (2.0 - den * guess)
                coded = (scale[at] * (1.0 / SHARP)) * (num * guess)
                dst[at, cols] = coded.astype(jnp.bfloat16)
            return later

        lax.fori_loop(0, blocks, one, scales(0), unroll=4)

    def over_blocks(body, init=0, wide=BLOCK):
        return lax.fori_loop(
            0, width // wide, lambda b, c: body(pl.ds(pl.multiple_of(b * wide, wide), wide), c), init
        )

    f32 = jnp.float32
    from_sib_copies, from_chip_copies = {}, {}

    def pair_sum(s):
        from_sib_copies[s].wait_recv()
        if s == 0:
            return

        def body(cols, c):
            coded_own[s, :, cols] = (
                coded_own[s, :, cols].astype(f32) + from_sib[s, :, cols].astype(f32)
            ).astype(jnp.bfloat16)
            return c

        over_blocks(body, wide=math.gcd(width, 2 * BLOCK))
        from_chip_copies[s] = send(
            coded_own.at[s], from_chip.at[s - 1], chip_send.at[s - 1], chip_recv.at[s - 1], peer[s]
        )

    for s in order:
        for v, dst in ((2 * s, coded_sib.at[s]), (2 * s + 1, coded_own.at[s])):
            for load in loads[v]:
                load.wait()
            encode(v, dst)
            if v % 2 == 0:
                from_sib_copies[s] = send(
                    coded_sib.at[s], from_sib.at[s], sib_send.at[s], sib_recv.at[s], sibling
                )
        pair_sum(s)
    for s in order[:-1]:
        from_chip_copies[s].wait_recv()

    def add_up(cols, acc):
        total = coded_own[0, :, cols].astype(f32) + from_sib[0, :, cols].astype(f32)
        for s in range(1, chips):
            total = total + from_chip[s - 1, :, cols].astype(f32)
        mean = total / f32(reps)
        mean_v[:, cols] = mean
        return acc + jnp.sum((mean * mean).reshape(rows // 8, 8, BLOCK), axis=0)

    parts[0] = over_blocks(add_up, jnp.zeros((8, BLOCK), f32))
    slot = 2
    sem = 0
    for stage, who in enumerate((near_by, across[1:])):
        copies = []
        for i, one in enumerate(who):
            copies.append(
                send(parts.at[stage], parts.at[slot + i], part_send.at[sem + i], part_recv.at[sem + i], one)
            )
        total = parts[stage]
        for i, copy in enumerate(copies):
            copy.wait()
            total = total + parts[slot + i]
        slot += len(who)
        sem += len(who)
        if stage < 1:
            parts[stage + 1] = total
    squares = jnp.full((8, BLOCK), jnp.sum(total))
    clip = jnp.max(
        jnp.minimum(f32(1.0), clip_rms / jnp.sqrt(squares / f32(entries) + 1e-06))
    )

    tall = rows // CHUNKS
    axes = [1 << i for i in range(chips.bit_length() - 1)]
    mom_in.wait()
    own_copies, fwd_copies, outs = {}, {}, []

    def spread(m, c):
        at = pl.ds(c * tall, tall)
        for h in axes:
            s = m | h
            over = [bit for bit in axes if s & bit]
            if s != m and over[c % len(over)] == h:
                i = (s - 1) * CHUNKS + c
                own_copies[s, c] = send(
                    half_v.at[2 * m + 1, at], half_v.at[2 * s + 1, at],
                    own_send.at[i], own_recv.at[i], peer[h],
                )

    def forward(s, c):
        v = 2 * s + 1
        at = pl.ds(c * tall, tall)
        fwd_copies[s, c] = send(
            half_v.at[v, at], half_v.at[v - 1, at],
            fwd_send.at[s * CHUNKS + c], fwd_recv.at[s * CHUNKS + c], sibling,
        )

    def mix(v, c):
        at = pl.ds(c * tall, tall)

        def body(cols, carry):
            inner_v[v, at, cols] = (
                mix_rate * half_v[v, at, cols].astype(f32)
                + (1.0 - mix_rate) * inner_v[v, at, cols].astype(f32)
            ).astype(jnp.bfloat16)
            return carry

        over_blocks(body, wide=broad)
        out = pltpu.make_async_copy(
            inner_v.at[v, at], next_hbm.at[0, at, columns(v)], out_sem.at[v * CHUNKS + c]
        )
        out.start()
        outs.append(out)

    for c in range(CHUNKS):
        at = pl.ds(c * tall, tall)

        def step(cols, carry):
            grad = clip * mean_v[at, cols]
            mom = outer_mu * mom_v[at, cols] + grad
            new = outer_v[1, at, cols] - outer_rate * (grad + outer_mu * mom)
            mom_out[at, cols] = mom
            outer_out[at, cols] = new
            half_v[1, at, cols] = new.astype(jnp.bfloat16)
            return carry

        over_blocks(step, wide=math.gcd(width, 4 * BLOCK))
        spread(0, c)
        forward(0, c)
    for i, (src, dst) in enumerate(((mom_out, mom_next_hbm), (outer_out, outer_next_hbm))):
        out = pltpu.make_async_copy(src, dst, flat_sem.at[i])
        out.start()
        outs.append(out)
    for c in range(CHUNKS):
        mix(1, c)
    for c in range(CHUNKS):
        fwd_copies[0, c].wait_recv()
        mix(0, c)
    last = None
    arrivals = [(s, c) for c in range(CHUNKS) for s in range(1, chips)]
    for s, c in sorted(arrivals, key=lambda sc: (sc[1] + bin(sc[0]).count("1"), sc)):
        own_copies[s, c].wait_recv()
        spread(s, c)
        forward(s, c)
        mix(2 * s + 1, c)
        if last is not None:
            fwd_copies[last].wait_recv()
            mix(2 * last[0], last[1])
        last = (s, c)
    if last is not None:
        fwd_copies[last].wait_recv()
        mix(2 * last[0], last[1])

    for copies in (from_sib_copies, from_chip_copies, own_copies, fwd_copies):
        for copy in copies.values():
            copy.wait_send()
    for out in outs:
        out.wait()


def per_device(inner, outer, momentum, exponents, levels):
    reps = lax.axis_size("rep")
    groups = lax.axis_size("fsdp")
    chips = reps // 2
    rows, columns = outer.shape
    width = momentum.shape[1]
    n_parts = (reps - 1) + (groups - 1)
    bf16, f32 = jnp.bfloat16, jnp.float32
    dma = pltpu.SemaphoreType.DMA
    hbm = pl.BlockSpec(memory_space=pl.ANY)
    return pl.pallas_call(
        functools.partial(kernel, reps, groups, rows * groups * columns),
        out_shape=(
            jax.ShapeDtypeStruct(inner.shape, inner.dtype),
            jax.ShapeDtypeStruct(momentum.shape, f32),
            jax.ShapeDtypeStruct(momentum.shape, f32),
        ),
        in_specs=[hbm] * 4 + [pl.BlockSpec(memory_space=pltpu.SMEM)],
        out_specs=(hbm,) * 3,
        scratch_shapes=[
            pltpu.VMEM((reps, rows, width), bf16),
            pltpu.VMEM((reps, rows, width), f32),
            pltpu.VMEM((rows, width), f32),
            pltpu.VMEM(exponents.shape[1:], jnp.int32),
            pltpu.VMEM((2,) + exponents.shape[1:], bf16),
            pltpu.VMEM((chips, rows, width), bf16),
            pltpu.VMEM((chips, rows, width), bf16),
            pltpu.VMEM((chips, rows, width), bf16),
            pltpu.VMEM((chips - 1, rows, width), bf16),
            pltpu.VMEM((rows, width), f32),
            pltpu.VMEM((reps, rows, width), bf16),
            pltpu.VMEM((rows, width), f32),
            pltpu.VMEM((rows, width), f32),
            pltpu.VMEM((2 + n_parts, 8, BLOCK), f32),
            dma((2 * reps + 2,)),
            dma((chips,)),
            dma((chips,)),
            dma((chips - 1,)),
            dma((chips - 1,)),
            dma((n_parts,)),
            dma((n_parts,)),
            dma(((chips - 1) * CHUNKS,)),
            dma(((chips - 1) * CHUNKS,)),
            dma((chips * CHUNKS,)),
            dma((chips * CHUNKS,)),
            dma((reps * CHUNKS,)),
            dma((2,)),
        ],
        compiler_params=pltpu.CompilerParams(
            collective_id=0, has_side_effects=True, vmem_limit_bytes=56 * 1024 * 1024
        ),
        cost_estimate=pl.CostEstimate(
            flops=100 * rows * columns,
            bytes_accessed=8 * rows * columns + 16 * rows * width,
            transcendentals=NLEV * rows * columns,
        ),
    )(inner, outer, momentum, exponents, levels)


def solution(mesh):
    placed = (
        P("rep", "fsdp", None),
        P("fsdp", None),
        P("fsdp", "rep"),
        P("rep", "fsdp", None),
        P(),
    )
    return jax.shard_map(
        per_device,
        mesh=mesh,
        in_specs=placed,
        out_specs=(P("rep", "fsdp", None), P("fsdp", "rep"), P("fsdp", "rep")),
        check_vma=False,
    )
```
